32 devices in a mesh: group: 2 (over x), patch: 8 (over z, y), tensor: 2 (over core).
Axes of the slice: x: 2, y: 2, z: 4, core: 2. Of those that a mesh axis runs over, the one named last changes fastest.
Arguments:
- hidden: bfloat16 [2, 1152, 3072], P(None, ('group', 'patch')), parts along dimension 1, may hold values from -6 to 6
- w_q: bfloat16 [3072, 1536], P(None, 'tensor'), may hold values from -0.109375 to 0.109375
- fresh_kv: bfloat16 [2, 1152, 2, 1536], P(None, ('group', 'patch'), None, 'tensor'), parts along dimension 1, may hold values from -6 to 6
- prev_kv: bfloat16 [1152, 2, 1536], P(('group', 'patch'), None, 'tensor'), parts along dimension 0, may hold values from -6 to 6
- exps: int32 [1152, 2, 12], P(('group', 'patch'), None, 'tensor'), parts along dimension 0, may hold values from 0 to 2
- w_out: bfloat16 [1536, 3072], P('tensor'), may hold values from -0.15625 to 0.15625
Outputs:
- mixed: bfloat16 [2, 1152, 3072], P(None, ('group', 'patch'), 'tensor'), parts along dimension 1
The draws below stay inside these ranges and needn't reach their ends.
There are 2 independent parts, one for each index of `group`. The reference program is written for one: setup_inputs(seed, part) draws one part's arguments, and reference() takes and returns one part's arrays. A program takes and returns all parts, laid end to end along the dimension named above; an argument that names none is the same for every part. Nothing has to cross between parts.
All inputs are finite; a program needn't handle non-finite values.
Results may differ from the reference program's by a relative error of at most 0.008.
Values may be sent and summed in bfloat16 or wider, within the bound.
A program may use at most 128 MiB of HBM per device.

```python
import jax
import jax.numpy as jnp
from jax import lax

D = 3072
HEADS = 12
HD = 128
TOK_DEV = 72
STEPS = 2
TOKENS = 576
N_PATCH = 8


def with_ends(entries, stream_key, smallest, top_value):
    dims = entries.shape
    index_at = [jax.random.randint(jax.random.fold_in(stream_key, axis), (), 0, dims[axis]) for axis in range(len(dims))]
    entries = entries.at[tuple(index_at)].set(smallest)
    longest = dims.index(max(dims))
    index_at[longest] = (index_at[longest] + 1) % dims[longest]
    return entries.at[tuple(index_at)].set(top_value)


def block_levels(own_key, shape, cuts, low, high):
    level, own = 1.0, jax.random.fold_in(own_key, 6)
    for dim, parts in cuts:
        steps = jnp.exp(jax.random.uniform(jax.random.fold_in(own, dim), (parts,), jnp.float32, low / len(cuts), high / len(cuts)))
        level = level * jnp.repeat(steps, shape[dim] // parts).reshape([-1 if axis == dim else 1 for axis in range(len(shape))])
    return level


def bell_draw(stream_key, dims, spread, limit, cuts=(), kind=jnp.bfloat16):
    array = spread * jax.random.normal(stream_key, dims, jnp.float32)
    if cuts:
        array = array * block_levels(stream_key, dims, cuts, -0.22, 0.18)
    return jnp.clip(array, -limit, limit).astype(kind)


def setup_inputs(seed: int = 0, part: int = 0) -> dict:
    seeds = jax.random.split(jax.random.key(seed), 7)
    own_keys = jax.random.split(jax.random.fold_in(seeds[6], part), 7)
    return {
        "hidden": bell_draw(own_keys[0], (STEPS, TOKENS, D), 1.0, 6.0, ((1, 8),)),
        "w_q": bell_draw(seeds[1], (D, HEADS * HD), D ** -0.5, 0.109375, ((1, 2),)),
        "fresh_kv": bell_draw(own_keys[2], (STEPS, TOKENS, 2, HEADS * HD), 1.0, 6.0, ((1, 8), (3, 2))),
        "prev_kv": bell_draw(own_keys[3], (TOKENS, 2, HEADS * HD), 1.0, 6.0, ((0, 8), (2, 2))),
        "exps": with_ends(jax.random.randint(own_keys[4], (TOKENS, 2, HEADS), 0, 3), jax.random.fold_in(own_keys[4], 1), 0, 2).astype(jnp.int32),
        "w_out": bell_draw(seeds[5], (HEADS * HD, D), (HEADS * HD) ** -0.5, 0.15625, ((0, 2),)),
    }


clip_limit = 1.0


def attend(queries, key_table, head_count):
    head_size = queries.shape[1] // head_count
    key_rows = key_table.shape[0]
    query_heads = queries.astype(jnp.float32).reshape(queries.shape[0], head_count, head_size)
    key_heads = key_table[:, 0].astype(jnp.float32).reshape(key_rows, head_count, head_size)
    value_heads = key_table[:, 1].astype(jnp.float32).reshape(key_rows, head_count, head_size)
    scores = jnp.einsum("qhd,khd->hqk", query_heads, key_heads) * (head_size ** -0.5)
    weights = jax.nn.softmax(scores, axis=-1).astype(jnp.bfloat16)
    result = jnp.einsum("hqk,khd->qhd", weights.astype(jnp.float32), value_heads)
    return result.astype(jnp.bfloat16).reshape(queries.shape)


def reference(hidden, w_q, fresh_kv, prev_kv, exps, w_out):
    query = jnp.einsum("std,de->ste", hidden.astype(jnp.float32), w_q.astype(jnp.float32)).astype(jnp.bfloat16)
    factor = jnp.repeat(jnp.exp2(-exps.astype(jnp.float32)), HD, axis=2)
    scaled = jnp.clip((fresh_kv[0].astype(jnp.float32) - prev_kv.astype(jnp.float32)) * factor, -clip_limit, clip_limit).astype(jnp.bfloat16)
    update = (scaled.astype(jnp.float32) / factor).astype(jnp.bfloat16)
    copy_kv = (prev_kv.astype(jnp.float32) + update.astype(jnp.float32)).astype(jnp.bfloat16)
    tables = (prev_kv, copy_kv)

    def one_shard(index):
        own_start = (index * TOK_DEV).astype(jnp.int32)
        results = []
        for step in range(STEPS):
            own_rows = lax.dynamic_slice_in_dim(fresh_kv[step], own_start, TOK_DEV, 0)
            key_table = lax.dynamic_update_slice_in_dim(tables[step], own_rows, own_start, 0)
            queries = lax.dynamic_slice_in_dim(query[step], own_start, TOK_DEV, 0)
            results.append(attend(queries, key_table, HEADS))
        return jnp.stack(results)

    attended = lax.map(one_shard, jnp.arange(N_PATCH, dtype=jnp.int32))
    attended = jnp.transpose(attended, (1, 0, 2, 3)).reshape(STEPS, TOKENS, HEADS * HD)
    mixed = jnp.einsum("ste,ed->std", attended.astype(jnp.float32), w_out.astype(jnp.float32))
    return mixed.astype(jnp.bfloat16)
```

```python
import functools

import jax
import jax.numpy as jnp
from jax import lax
from jax.experimental import pallas as pl
from jax.experimental.pallas import tpu as pltpu
from jax.sharding import PartitionSpec as P

HD = 128
STEPS = 2
CLIP = 1.0
MESH = pl.DeviceIdType.MESH
F32 = jnp.float32
BF16 = jnp.bfloat16
DOWN, UP, LEFT, RIGHT = 0, 1, 2, 3


def grid_of(count):
    columns = 1
    while columns * columns * 4 <= count and count % (columns * 2) == 0:
        columns *= 2
    return count // columns, columns


def kernel(
    rows, cols,
    hidden, w_q, fresh, prev, exps, w_out,
    out,
    hid, wq, wo_own, wo_far, query, table, copy_own, probs, att, att_far,
    local_sem, send_sem, recv_sem, core_send, core_recv, att_send, att_recv,
):
    tok, width = prev.shape[1], prev.shape[2]
    heads = width // HD
    n = rows * cols
    keys = n * tok
    half = w_out.shape[1] // 2
    me = lax.axis_index("patch")
    core = lax.axis_index("tensor")
    row, col = me // cols, me % cols
    q_parts = wq.shape[0]

    barrier = pltpu.get_barrier_semaphore()
    near = [
        (row > 0, me - cols), (row < rows - 1, me + cols),
        (col > 0, me - 1), (col < cols - 1, me + 1),
    ]
    count = jnp.int32(1)
    for here, index in near:
        @pl.when(here)
        def _(index=index):
            pl.semaphore_signal(barrier, inc=1, device_id={"patch": index}, device_id_type=MESH)
        count = count + here.astype(jnp.int32)
    pl.semaphore_signal(barrier, inc=1, device_id={"tensor": 1 - core}, device_id_type=MESH)

    local = [pltpu.make_async_copy(hidden, hid, local_sem.at[0])]
    part = width // q_parts
    for j in range(q_parts):
        local.append(
            pltpu.make_async_copy(w_q.at[:, pl.ds(j * part, part)], wq.at[j], local_sem.at[1 + j])
        )
    mine = pl.ds(pl.multiple_of(core * half, half), half)
    theirs = pl.ds(pl.multiple_of((1 - core) * half, half), half)
    for copy in local:
        copy.start()
    wo_copy = pltpu.make_async_copy(w_out.at[:, mine], wo_own, local_sem.at[1 + q_parts])
    wo_copy.start()
    pl.semaphore_wait(barrier, count)

    sent = []

    def remote(src, chunk, block, way):
        index = (me - cols, me + cols, me - 1, me + 1)[way]
        return pltpu.make_async_remote_copy(
            src_ref=src, dst_ref=table.at[chunk, block],
            send_sem=send_sem.at[chunk, block, way], recv_sem=recv_sem.at[chunk, block],
            device_id={"patch": index}, device_id_type=MESH,
        )

    def push(src, chunk, block, way, when):
        @pl.when(when)
        def _():
            remote(src, chunk, block, way).start()

    ways_row = ((DOWN, row > 0), (UP, row < rows - 1))
    ways_col = ((LEFT, col > 0), (RIGHT, col < cols - 1))

    def own_src(chunk):
        return prev.at[chunk] if chunk < 2 else copy_own.at[chunk - 2]

    def send_own(chunk):
        for way, when in ways_row + ways_col:
            push(own_src(chunk), chunk, me, way, when)

    def landed(chunk, block):
        remote(table.at[chunk, block], chunk, block, UP).wait_recv()

    def row_events(chunk):
        for d in range(1, rows):
            for way, when, src_row in ((UP, row >= d, row - d), (DOWN, row + d < rows, row + d)):
                @pl.when(when)
                def _(way=way, src_row=src_row):
                    block = src_row * cols + col
                    landed(chunk, block)
                    slot = table.at[chunk, block]
                    for side, ok in ways_col:
                        push(slot, chunk, block, side, ok)
                    push(slot, chunk, block, way, ways_row[way][1])

    def col_events(chunk):
        for e in range(1, cols):
            for k in range(rows):
                for way, when, src_col in ((RIGHT, col >= e, col - e), (LEFT, col + e < cols, col + e)):
                    @pl.when(when)
                    def _(way=way, src_col=src_col, k=k):
                        block = k * cols + src_col
                        landed(chunk, block)
                        if e < cols - 1:
                            push(table.at[chunk, block], chunk, block, way, ways_col[way - 2][1])

    def drain():
        for chunk in range(4):
            for way, when in ways_row + ways_col:
                @pl.when(when)
                def _(way=way, chunk=chunk):
                    remote(own_src(chunk), chunk, me, way).wait_send()
            for d in range(1, rows):
                for way, when, src_row in ((UP, row >= d, row - d), (DOWN, row + d < rows, row + d)):
                    for side, ok in ways_col + (ways_row[way],):
                        @pl.when(jnp.logical_and(when, ok))
                        def _(side=side, src_row=src_row, chunk=chunk):
                            block = src_row * cols + col
                            remote(table.at[chunk, block], chunk, block, side).wait_send()
            for e in range(1, cols - 1):
                for k in range(rows):
                    for way, when, src_col in ((RIGHT, col >= e, col - e), (LEFT, col + e < cols, col + e)):
                        @pl.when(jnp.logical_and(when, ways_col[way - 2][1]))
                        def _(way=way, src_col=src_col, k=k, chunk=chunk):
                            block = k * cols + src_col
                            remote(table.at[chunk, block], chunk, block, way).wait_send()

    send_own(0)
    send_own(1)
    far_copy = pltpu.make_async_remote_copy(
        src_ref=w_out.at[:, theirs], dst_ref=wo_far,
        send_sem=core_send, recv_sem=core_recv,
        device_id={"tensor": 1 - core}, device_id_type=MESH,
    )
    far_copy.start()

    for kv in range(2):
        for h in range(heads):
            at = slice(h * HD, (h + 1) * HD)
            factor = jnp.exp2(-exps[kv, :, h:h + 1].astype(F32))
            old = prev[kv, :, at].astype(F32)
            scaled = jnp.clip((fresh[0, kv, :, at].astype(F32) - old) * factor, -CLIP, CLIP).astype(BF16)
            update = (scaled.astype(F32) / factor).astype(BF16)
            copy_own[kv, :, at] = (old + update.astype(F32)).astype(BF16)
    send_own(2)
    for chunk in range(4):
        table[chunk, me] = fresh[chunk // 2, chunk % 2]

    local[0].wait()
    for j in range(q_parts):
        local[1 + j].wait()
        result = jnp.dot(hid[...], wq[j], preferred_element_type=F32).astype(BF16)
        query[0, :, j * part:(j + 1) * part] = result[:tok]
        query[1, :, j * part:(j + 1) * part] = result[tok:]

    def softmax(step, h):
        at = slice(h * HD, (h + 1) * HD)
        k_rows = table[2 * step, :, :, at].reshape(keys, HD)
        scores = lax.dot_general(
            query[step, :, at], k_rows, (((1,), (1,)), ((), ())), preferred_element_type=F32
        ) * HD ** -0.5
        e = jnp.exp(scores - jnp.max(scores, axis=1, keepdims=True))
        return (e / jnp.sum(e, axis=1, keepdims=True)).astype(BF16)

    def mix_values(step, h, weights):
        at = slice(h * HD, (h + 1) * HD)
        v_rows = table[2 * step + 1, :, :, at].reshape(keys, HD)
        att[step, :, at] = jnp.dot(weights, v_rows, preferred_element_type=F32).astype(BF16)

    def swap(step):
        return pltpu.make_async_remote_copy(
            src_ref=att.at[step], dst_ref=att_far.at[step],
            send_sem=att_send.at[step], recv_sem=att_recv.at[step],
            device_id={"tensor": 1 - core}, device_id_type=MESH,
        )

    tile = 512
    def project(step):
        swap(step).wait_recv()
        for j in range(half // tile):
            at = slice(j * tile, (j + 1) * tile)
            total = jnp.dot(att[step], wo_own[:, at], preferred_element_type=F32)
            total = total + jnp.dot(att_far[step], wo_far[:, at], preferred_element_type=F32)
            out[step, :, at] = total.astype(BF16)

    row_events(0)
    row_events(1)
    send_own(3)
    row_events(2)
    col_events(0)
    col_events(1)
    for h in range(heads):
        mix_values(0, h, softmax(0, h))
    swap(0).start()
    row_events(3)
    wo_copy.wait()
    far_copy.wait()
    col_events(2)
    for h in range(heads):
        probs[h] = softmax(1, h)
    project(0)
    col_events(3)
    for h in range(heads):
        mix_values(1, h, probs[h])
    swap(1).start()
    project(1)
    swap(0).wait_send()
    swap(1).wait_send()
    drain()


def on_device(rows, cols, hidden, w_q, fresh_kv, prev_kv, exps, w_out):
    tok, width = hidden.shape[1], w_q.shape[1]
    depth, half = w_q.shape[0], w_out.shape[1] // 2
    n = rows * cols
    fresh = jnp.transpose(fresh_kv, (0, 2, 1, 3))
    prev = jnp.transpose(prev_kv, (1, 0, 2))
    powers = jnp.transpose(exps, (1, 0, 2))
    q_parts = 3
    vmem = pl.BlockSpec(memory_space=pltpu.VMEM)
    anywhere = pl.BlockSpec(memory_space=pl.ANY)
    dma = pltpu.SemaphoreType.DMA
    return pl.pallas_call(
        functools.partial(kernel, rows, cols),
        out_shape=jax.ShapeDtypeStruct((STEPS, tok, half), BF16),
        in_specs=[anywhere, anywhere, vmem, vmem, vmem, anywhere],
        out_specs=vmem,
        scratch_shapes=[
            pltpu.VMEM((STEPS * tok, depth), BF16),
            pltpu.VMEM((q_parts, depth, width // q_parts), BF16),
            pltpu.VMEM((width, half), BF16),
            pltpu.VMEM((width, half), BF16),
            pltpu.VMEM((STEPS, tok, width), BF16),
            pltpu.VMEM((2 * STEPS, n, tok, width), BF16),
            pltpu.VMEM((2, tok, width), BF16),
            pltpu.VMEM((width // HD, tok, n * tok), BF16),
            pltpu.VMEM((STEPS, tok, width), BF16),
            pltpu.VMEM((STEPS, tok, width), BF16),
            dma((2 + q_parts,)),
            dma((2 * STEPS, n, 4)),
            dma((2 * STEPS, n)),
            dma,
            dma,
            dma((STEPS,)),
            dma((STEPS,)),
        ],
        compiler_params=pltpu.CompilerParams(
            collective_id=0, has_side_effects=True, vmem_limit_bytes=60 * 2**20
        ),
    )(hidden.reshape(STEPS * tok, depth), w_q, fresh, prev, powers, w_out)


def solution(mesh):
    rows, cols = grid_of(mesh.shape["patch"])
    return jax.shard_map(
        functools.partial(on_device, rows, cols),
        mesh=mesh,
        in_specs=(
            P(None, ("group", "patch"), None),
            P(None, "tensor"),
            P(None, ("group", "patch"), None, "tensor"),
            P(("group", "patch"), None, "tensor"),
            P(("group", "patch"), None, "tensor"),
            P("tensor", None),
        ),
        out_specs=P(None, ("group", "patch"), "tensor"),
        check_vma=False,
    )
```

```python
import functools

import jax
import jax.numpy as jnp
from jax import lax
from jax.experimental import pallas as pl
from jax.experimental.pallas import tpu as pltpu
from jax.sharding import PartitionSpec as P

HD = 128
STEPS = 2
CLIP = 1.0
MESH = pl.DeviceIdType.MESH
F32 = jnp.float32
BF16 = jnp.bfloat16
DOWN, UP = 0, 1


def grid_of(count):
    columns = 1
    while columns * columns * 4 <= count and count % (columns * 2) == 0:
        columns *= 2
    return count // columns, columns


def kernel(
    rows, cols,
    hidden, w_q, fresh, prev, exps, w_out,
    out,
    hid, wq, wo_own, wo_far, query, query_in, table, probs, own_sum, own_stat,
    part_out, stat_out, part_in, stat_in, att, att_far,
    local_sem, send_sem, recv_sem, core_send, core_recv, att_send, att_recv,
    query_send, query_recv, part_send, part_recv, stat_send, stat_recv,
):
    tok, width = prev.shape[1], prev.shape[2]
    heads = width // HD
    keys = rows * tok
    half = w_out.shape[1] // 2
    me = lax.axis_index("patch")
    core = lax.axis_index("tensor")
    row, col = me // cols, me % cols
    q_parts = wq.shape[0]
    peers = range(1, cols)

    def peer(j):
        return row * cols + lax.rem(col + j + cols, cols)

    barrier = pltpu.get_barrier_semaphore()
    count = jnp.int32(cols)
    for here, index in ((row > 0, me - cols), (row < rows - 1, me + cols)):
        @pl.when(here)
        def _(index=index):
            pl.semaphore_signal(barrier, inc=1, device_id={"patch": index}, device_id_type=MESH)
        count = count + here.astype(jnp.int32)
    for j in peers:
        pl.semaphore_signal(barrier, inc=1, device_id={"patch": peer(j)}, device_id_type=MESH)
    pl.semaphore_signal(barrier, inc=1, device_id={"tensor": 1 - core}, device_id_type=MESH)

    local = [pltpu.make_async_copy(hidden, hid, local_sem.at[0])]
    part = width // q_parts
    for j in range(q_parts):
        local.append(
            pltpu.make_async_copy(w_q.at[:, pl.ds(j * part, part)], wq.at[j], local_sem.at[1 + j])
        )
    mine = pl.ds(pl.multiple_of(core * half, half), half)
    theirs = pl.ds(pl.multiple_of((1 - core) * half, half), half)
    for copy in local:
        copy.start()
    wo_copy = pltpu.make_async_copy(w_out.at[:, mine], wo_own, local_sem.at[1 + q_parts])
    wo_copy.start()
    pl.semaphore_wait(barrier, count)

    def remote(src, chunk, src_row, way):
        to = row + (-1, 1)[way]
        slot = lax.rem(src_row - to + 2 * rows, rows)
        return pltpu.make_async_remote_copy(
            src_ref=src, dst_ref=table.at[chunk, slot],
            send_sem=send_sem.at[chunk, lax.rem(src_row - row + rows, rows), way],
            recv_sem=recv_sem.at[chunk, slot],
            device_id={"patch": to * cols + col}, device_id_type=MESH,
        )

    may = (row > 0, row < rows - 1)

    def own_src(chunk):
        return prev.at[chunk] if chunk < 2 else table.at[chunk, rows]

    def send_own(chunk):
        for way in (DOWN, UP):
            @pl.when(may[way])
            def _(way=way):
                remote(own_src(chunk), chunk, row, way).start()

    def sides(d):
        return ((UP, row >= d, -d % rows, row - d), (DOWN, row + d < rows, d, row + d))

    def row_events(chunk, distances):
        for d in distances:
            for way, when, slot, src_row in sides(d):
                @pl.when(when)
                def _(way=way, slot=slot, src_row=src_row):
                    here = table.at[chunk, slot]
                    pltpu.make_async_remote_copy(
                        src_ref=here, dst_ref=here,
                        send_sem=send_sem.at[chunk, slot, way], recv_sem=recv_sem.at[chunk, slot],
                        device_id={"patch": me}, device_id_type=MESH,
                    ).wait_recv()

                    @pl.when(may[way])
                    def _():
                        remote(here, chunk, src_row, way).start()

    def drain():
        for chunk in range(2 * STEPS):
            for way in (DOWN, UP):
                @pl.when(may[way])
                def _(way=way, chunk=chunk):
                    remote(own_src(chunk), chunk, row, way).wait_send()
            for d in range(1, rows):
                for way, when, slot, src_row in sides(d):
                    @pl.when(jnp.logical_and(when, may[way]))
                    def _(way=way, slot=slot, src_row=src_row, chunk=chunk):
                        remote(table.at[chunk, slot], chunk, src_row, way).wait_send()

    send_own(0)
    send_own(1)
    far_copy = pltpu.make_async_remote_copy(
        src_ref=w_out.at[:, theirs], dst_ref=wo_far,
        send_sem=core_send, recv_sem=core_recv,
        device_id={"tensor": 1 - core}, device_id_type=MESH,
    )
    far_copy.start()

    for kv in range(2):
        table[kv, rows] = prev[kv]
        for h in range(heads):
            at = slice(h * HD, (h + 1) * HD)
            factor = jnp.exp2(-exps[kv, :, h:h + 1].astype(F32))
            old = prev[kv, :, at].astype(F32)
            scaled = jnp.clip((fresh[0, kv, :, at].astype(F32) - old) * factor, -CLIP, CLIP).astype(BF16)
            update = (scaled.astype(F32) / factor).astype(BF16)
            table[2 + kv, rows, :, at] = (old + update.astype(F32)).astype(BF16)
    send_own(2)
    for chunk in range(2 * STEPS):
        table[chunk, 0] = fresh[chunk // 2, chunk % 2]

    local[0].wait()
    for j in range(q_parts):
        local[1 + j].wait()
        result = jnp.dot(hid[...], wq[j], preferred_element_type=F32).astype(BF16)
        query[0, :, j * part:(j + 1) * part] = result[:tok]
        query[1, :, j * part:(j + 1) * part] = result[tok:]

    def query_copy(j):
        return pltpu.make_async_remote_copy(
            src_ref=query, dst_ref=query_in.at[j], send_sem=query_send.at[j], recv_sem=query_recv.at[j],
            device_id={"patch": peer(j)}, device_id_type=MESH,
        )

    def part_copies(step, j):
        return [
            pltpu.make_async_remote_copy(
                src_ref=src.at[step, j], dst_ref=dst.at[step, j],
                send_sem=send.at[step, j], recv_sem=recv.at[step, j],
                device_id={"patch": peer(-j)}, device_id_type=MESH,
            )
            for src, dst, send, recv in (
                (part_out, part_in, part_send, part_recv), (stat_out, stat_in, stat_send, stat_recv),
            )
        ]

    for j in peers:
        query_copy(j).start()

    def at_head(h):
        return slice(h * HD, (h + 1) * HD)

    def weigh(step, h, j):
        first = 1 if j else 0
        queries = query_in[j, step, :, at_head(h)] if j else query[step, :, at_head(h)]
        k_rows = table[2 * step, first:first + rows, :, at_head(h)].reshape(keys, HD)
        scores = lax.dot_general(
            queries, k_rows, (((1,), (1,)), ((), ())), preferred_element_type=F32
        ) * HD ** -0.5
        top = jnp.max(scores, axis=1, keepdims=True)
        e = jnp.exp(scores - top)
        probs[j, h] = e.astype(BF16)
        total = jnp.sum(e, axis=1, keepdims=True)
        if j:
            stat_out[step, j, :, h:h + 1] = top
            stat_out[step, j, :, heads + h:heads + h + 1] = total
        else:
            own_stat[:, h:h + 1] = top
            own_stat[:, heads + h:heads + h + 1] = total

    def mix_values(step, h, j):
        first = 1 if j else 0
        v_rows = table[2 * step + 1, first:first + rows, :, at_head(h)].reshape(keys, HD)
        mixed = jnp.dot(probs[j, h], v_rows, preferred_element_type=F32)
        if j:
            total = stat_out[step, j, :, heads + h:heads + h + 1]
            part_out[step, j, :, at_head(h)] = (mixed / total).astype(BF16)
        else:
            own_sum[:, at_head(h)] = mixed

    def each_head(run, step, who):
        for j in who:
            for h in range(heads):
                run(step, h, j)

    def give_back(step):
        for j in peers:
            for copy in part_copies(step, j):
                copy.start()

    def merge(step):
        for j in peers:
            for copy in part_copies(step, j):
                copy.wait_recv()
        for h in range(heads):
            one, two = slice(h, h + 1), slice(heads + h, heads + h + 1)
            top = own_stat[:, one]
            for j in peers:
                top = jnp.maximum(top, stat_in[step, j, :, one])
            share = jnp.exp(own_stat[:, one] - top)
            below = own_stat[:, two] * share
            above = own_sum[:, at_head(h)] * share
            for j in peers:
                share = stat_in[step, j, :, two] * jnp.exp(stat_in[step, j, :, one] - top)
                below = below + share
                above = above + part_in[step, j, :, at_head(h)].astype(F32) * share
            att[step, :, at_head(h)] = (above / below).astype(BF16)

    def swap(step):
        return pltpu.make_async_remote_copy(
            src_ref=att.at[step], dst_ref=att_far.at[step],
            send_sem=att_send.at[step], recv_sem=att_recv.at[step],
            device_id={"tensor": 1 - core}, device_id_type=MESH,
        )

    tile = 512

    def project(step):
        swap(step).wait_recv()
        for j in range(half // tile):
            at = slice(j * tile, (j + 1) * tile)
            total = jnp.dot(att[step], wo_own[:, at], preferred_element_type=F32)
            total = total + jnp.dot(att_far[step], wo_far[:, at], preferred_element_type=F32)
            out[step, :, at] = total.astype(BF16)

    every = range(1, rows)
    row_events(0, every)
    send_own(3)
    row_events(1, every)
    for j in peers:
        query_copy(j).wait_recv()
    each_head(weigh, 0, peers)
    each_head(mix_values, 0, peers)
    give_back(0)
    row_events(2, every)
    each_head(weigh, 0, (0,))
    each_head(mix_values, 0, (0,))
    row_events(3, every[:1])
    merge(0)
    swap(0).start()
    each_head(weigh, 1, peers)
    row_events(3, every[1:2])
    each_head(weigh, 1, (0,))
    wo_copy.wait()
    far_copy.wait()
    project(0)
    row_events(3, every[2:])
    each_head(mix_values, 1, peers)
    give_back(1)
    each_head(mix_values, 1, (0,))
    merge(1)
    swap(1).start()
    project(1)
    for step in range(STEPS):
        swap(step).wait_send()
        for j in peers:
            for copy in part_copies(step, j):
                copy.wait_send()
    for j in peers:
        query_copy(j).wait_send()
    drain()


def on_device(rows, cols, hidden, w_q, fresh_kv, prev_kv, exps, w_out):
    tok, width = hidden.shape[1], w_q.shape[1]
    depth, half = w_q.shape[0], w_out.shape[1] // 2
    heads = width // HD
    fresh = jnp.transpose(fresh_kv, (0, 2, 1, 3))
    prev = jnp.transpose(prev_kv, (1, 0, 2))
    powers = jnp.transpose(exps, (1, 0, 2))
    q_parts = 3
    vmem = pl.BlockSpec(memory_space=pltpu.VMEM)
    anywhere = pl.BlockSpec(memory_space=pl.ANY)
    dma = pltpu.SemaphoreType.DMA
    return pl.pallas_call(
        functools.partial(kernel, rows, cols),
        out_shape=jax.ShapeDtypeStruct((STEPS, tok, half), BF16),
        in_specs=[anywhere, anywhere, vmem, vmem, vmem, anywhere],
        out_specs=vmem,
        scratch_shapes=[
            pltpu.VMEM((STEPS * tok, depth), BF16),
            pltpu.VMEM((q_parts, depth, width // q_parts), BF16),
            pltpu.VMEM((width, half), BF16),
            pltpu.VMEM((width, half), BF16),
            pltpu.VMEM((STEPS, tok, width), BF16),
            pltpu.VMEM((cols, STEPS, tok, width), BF16),
            pltpu.VMEM((2 * STEPS, rows + 1, tok, width), BF16),
            pltpu.VMEM((cols, heads, tok, rows * tok), BF16),
            pltpu.VMEM((tok, width), F32),
            pltpu.VMEM((tok, HD), F32),
            pltpu.VMEM((STEPS, cols, tok, width), BF16),
            pltpu.VMEM((STEPS, cols, tok, HD), F32),
            pltpu.VMEM((STEPS, cols, tok, width), BF16),
            pltpu.VMEM((STEPS, cols, tok, HD), F32),
            pltpu.VMEM((STEPS, tok, width), BF16),
            pltpu.VMEM((STEPS, tok, width), BF16),
            dma((2 + q_parts,)),
            dma((2 * STEPS, rows, 2)),
            dma((2 * STEPS, rows)),
            dma,
            dma,
            dma((STEPS,)),
            dma((STEPS,)),
            dma((cols,)),
            dma((cols,)),
            dma((STEPS, cols)),
            dma((STEPS, cols)),
            dma((STEPS, cols)),
            dma((STEPS, cols)),
        ],
        compiler_params=pltpu.CompilerParams(
            collective_id=0, has_side_effects=True, vmem_limit_bytes=60 * 2**20
        ),
    )(hidden.reshape(STEPS * tok, depth), w_q, fresh, prev, powers, w_out)


def solution(mesh):
    rows, cols = grid_of(mesh.shape["patch"])
    return jax.shard_map(
        functools.partial(on_device, rows, cols),
        mesh=mesh,
        in_specs=(
            P(None, ("group", "patch"), None),
            P(None, "tensor"),
            P(None, ("group", "patch"), None, "tensor"),
            P(("group", "patch"), None, "tensor"),
            P(("group", "patch"), None, "tensor"),
            P("tensor", None),
        ),
        out_specs=P(None, ("group", "patch"), "tensor"),
        check_vma=False,
    )
```

```python
import functools

import jax
import jax.numpy as jnp
from jax import lax
from jax.experimental import pallas as pl
from jax.experimental.pallas import tpu as pltpu
from jax.sharding import PartitionSpec as P

HD = 128
STEPS = 2
CLIP = 1.0
MESH = pl.DeviceIdType.MESH
F32 = jnp.float32
BF16 = jnp.bfloat16
QUAD = 4
BY_ROW = ()


def grid_of(count):
    columns = 1
    while columns * columns * 4 <= count and count % (columns * 2) == 0:
        columns *= 2
    return count // columns, columns


def kernel(
    rows, cols,
    hidden, w_q, fresh, prev, exps, w_out,
    out,
    hid, wq, wo_own, wo_far, query, query_in, table, probs, own_sum, own_stat,
    part_out, stat_out, part_in, stat_in, att, att_far,
    local_sem, send_sem, recv_sem, core_send, core_recv, att_send, att_recv,
    query_send, query_recv, part_send, part_recv, stat_send, stat_recv,
):
    tok, width = prev.shape[1], prev.shape[2]
    heads = width // HD
    keys = QUAD * tok
    half = w_out.shape[1] // 2
    me = lax.axis_index("patch")
    core = lax.axis_index("tensor")
    row, col = me // cols, me % cols
    q_parts = wq.shape[0]
    groups = rows * cols // QUAD
    peers = range(1, groups)
    group = (row // 2) * (cols // 2) + col // 2
    row_peer = (row + 1 - 2 * (row % 2)) * cols + col
    col_peer = row * cols + col + 1 - 2 * (col % 2)

    def peer(j):
        to = lax.rem(group + j + groups, groups)
        return (2 * (to // (cols // 2)) + row % 2) * cols + 2 * (to % (cols // 2)) + col % 2

    barrier = pltpu.get_barrier_semaphore()
    for index in [row_peer, col_peer] + [peer(j) for j in peers]:
        pl.semaphore_signal(barrier, inc=1, device_id={"patch": index}, device_id_type=MESH)
    pl.semaphore_signal(barrier, inc=1, device_id={"tensor": 1 - core}, device_id_type=MESH)

    local = [pltpu.make_async_copy(hidden, hid, local_sem.at[0])]
    part = width // q_parts
    for j in range(q_parts):
        local.append(
            pltpu.make_async_copy(w_q.at[:, pl.ds(j * part, part)], wq.at[j], local_sem.at[1 + j])
        )
    mine = pl.ds(pl.multiple_of(core * half, half), half)
    theirs = pl.ds(pl.multiple_of((1 - core) * half, half), half)
    for copy in local:
        copy.start()
    wo_copy = pltpu.make_async_copy(w_out.at[:, mine], wo_own, local_sem.at[1 + q_parts])
    wo_copy.start()
    pl.semaphore_wait(barrier, groups + 2)

    def remote(src, chunk, slot, index):
        return pltpu.make_async_remote_copy(
            src_ref=src, dst_ref=table.at[chunk, slot],
            send_sem=send_sem.at[chunk, slot], recv_sem=recv_sem.at[chunk, slot],
            device_id={"patch": index}, device_id_type=MESH,
        )

    def own_copies(chunk):
        src = prev.at[chunk] if chunk < 2 else table.at[chunk, QUAD]
        return [remote(src, chunk, 2, col_peer), remote(src, chunk, 1, row_peer)]

    def onward(chunk):
        first, index = (2, row_peer) if chunk in BY_ROW else (1, col_peer)
        return first, remote(table.at[chunk, first], chunk, 3, index)

    def send_own(chunk):
        for copy in own_copies(chunk):
            copy.start()

    def forward(chunk):
        first, copy = onward(chunk)
        own_copies(chunk)[2 - first].wait_recv()
        copy.start()

    def complete(chunk):
        first, copy = onward(chunk)
        own_copies(chunk)[first - 1].wait_recv()
        copy.wait_recv()

    def drain():
        for chunk in range(2 * STEPS):
            for copy in own_copies(chunk) + [onward(chunk)[1]]:
                copy.wait_send()

    send_own(0)
    send_own(1)
    far_copy = pltpu.make_async_remote_copy(
        src_ref=w_out.at[:, theirs], dst_ref=wo_far,
        send_sem=core_send, recv_sem=core_recv,
        device_id={"tensor": 1 - core}, device_id_type=MESH,
    )
    far_copy.start()

    def query_copy(j):
        return pltpu.make_async_remote_copy(
            src_ref=query, dst_ref=query_in.at[j], send_sem=query_send.at[j], recv_sem=query_recv.at[j],
            device_id={"patch": peer(j)}, device_id_type=MESH,
        )

    def part_copies(step, j):
        return [
            pltpu.make_async_remote_copy(
                src_ref=src.at[step, j], dst_ref=dst.at[step, j],
                send_sem=send.at[step, j], recv_sem=recv.at[step, j],
                device_id={"patch": peer(-j)}, device_id_type=MESH,
            )
            for src, dst, send, recv in (
                (part_out, part_in, part_send, part_recv), (stat_out, stat_in, stat_send, stat_recv),
            )
        ]

    local[0].wait()
    for j in range(q_parts):
        local[1 + j].wait()
        result = jnp.dot(hid[...], wq[j], preferred_element_type=F32).astype(BF16)
        query[0, :, j * part:(j + 1) * part] = result[:tok]
        query[1, :, j * part:(j + 1) * part] = result[tok:]

    for j in peers:
        query_copy(j).start()

    for kv in range(2):
        table[kv, QUAD] = prev[kv]
        for h in range(heads):
            at = slice(h * HD, (h + 1) * HD)
            factor = jnp.exp2(-exps[kv, :, h:h + 1].astype(F32))
            old = prev[kv, :, at].astype(F32)
            scaled = jnp.clip((fresh[0, kv, :, at].astype(F32) - old) * factor, -CLIP, CLIP).astype(BF16)
            update = (scaled.astype(F32) / factor).astype(BF16)
            table[2 + kv, QUAD, :, at] = (old + update.astype(F32)).astype(BF16)
    for chunk in range(2 * STEPS):
        table[chunk, 0] = fresh[chunk // 2, chunk % 2]

    def at_head(h):
        return slice(h * HD, (h + 1) * HD)

    def weigh(step, h, j):
        other = not isinstance(j, int) or j > 0
        first = 1 if other else 0
        queries = query_in[j, step, :, at_head(h)] if other else query[step, :, at_head(h)]
        k_rows = table[2 * step, first:first + QUAD, :, at_head(h)].reshape(keys, HD)
        scores = lax.dot_general(
            queries, k_rows, (((1,), (1,)), ((), ())), preferred_element_type=F32
        ) * HD ** -0.5
        top = jnp.max(scores, axis=1, keepdims=True)
        e = jnp.exp(scores - top)
        probs[j, h] = e.astype(BF16)
        total = jnp.sum(e, axis=1, keepdims=True)
        if other:
            stat_out[step, j, :, h:h + 1] = top
            stat_out[step, j, :, heads + h:heads + h + 1] = total
        else:
            own_stat[:, h:h + 1] = top
            own_stat[:, heads + h:heads + h + 1] = total

    def mix_values(step, h, j):
        other = not isinstance(j, int) or j > 0
        first = 1 if other else 0
        v_rows = table[2 * step + 1, first:first + QUAD, :, at_head(h)].reshape(keys, HD)
        mixed = jnp.dot(probs[j, h], v_rows, preferred_element_type=F32)
        if other:
            total = stat_out[step, j, :, heads + h:heads + h + 1]
            part_out[step, j, :, at_head(h)] = (mixed / total).astype(BF16)
        else:
            own_sum[:, at_head(h)] = mixed

    def each_head(run, step, who):
        for j in who:
            for h in range(heads):
                run(step, h, j)

    def each_peer(runs, step):
        def body(j, carry):
            for run in runs:
                for h in range(heads):
                    run(step, h, j)
            return carry
        if groups == 2:
            body(1, 0)
        else:
            lax.fori_loop(1, groups, body, 0)

    def give_back(step):
        for j in peers:
            for copy in part_copies(step, j):
                copy.start()

    def merge(step):
        for j in peers:
            for copy in part_copies(step, j):
                copy.wait_recv()
        for h in range(heads):
            one, two = slice(h, h + 1), slice(heads + h, heads + h + 1)
            top = own_stat[:, one]
            for j in peers:
                top = jnp.maximum(top, stat_in[step, j, :, one])
            share = jnp.exp(own_stat[:, one] - top)
            below = own_stat[:, two] * share
            above = own_sum[:, at_head(h)] * share
            for j in peers:
                share = stat_in[step, j, :, two] * jnp.exp(stat_in[step, j, :, one] - top)
                below = below + share
                above = above + part_in[step, j, :, at_head(h)].astype(F32) * share
            att[step, :, at_head(h)] = (above / below).astype(BF16)

    def swap(step):
        return pltpu.make_async_remote_copy(
            src_ref=att.at[step], dst_ref=att_far.at[step],
            send_sem=att_send.at[step], recv_sem=att_recv.at[step],
            device_id={"tensor": 1 - core}, device_id_type=MESH,
        )

    tile = 512

    def project(step):
        swap(step).wait_recv()
        for j in range(half // tile):
            at = slice(j * tile, (j + 1) * tile)
            total = jnp.dot(att[step], wo_own[:, at], preferred_element_type=F32)
            total = total + jnp.dot(att_far[step], wo_far[:, at], preferred_element_type=F32)
            out[step, :, at] = total.astype(BF16)

    forward(0)
    send_own(2)
    forward(1)
    send_own(3)
    forward(2)
    complete(0)
    complete(1)
    for j in peers:
        query_copy(j).wait_recv()
    each_peer((weigh, mix_values), 0)
    give_back(0)
    forward(3)
    complete(2)
    each_peer((weigh,), 1)
    complete(3)
    each_peer((mix_values,), 1)
    give_back(1)
    each_head(weigh, 0, (0,))
    each_head(mix_values, 0, (0,))
    wo_copy.wait()
    far_copy.wait()
    merge(0)
    swap(0).start()
    each_head(weigh, 1, (0,))
    each_head(mix_values, 1, (0,))
    project(0)
    merge(1)
    swap(1).start()
    project(1)
    for step in range(STEPS):
        swap(step).wait_send()
        for j in peers:
            for copy in part_copies(step, j):
                copy.wait_send()
    for j in peers:
        query_copy(j).wait_send()
    drain()


def on_device(rows, cols, hidden, w_q, fresh_kv, prev_kv, exps, w_out):
    tok, width = hidden.shape[1], w_q.shape[1]
    depth, half = w_q.shape[0], w_out.shape[1] // 2
    heads = width // HD
    groups = rows * cols // QUAD
    fresh = jnp.transpose(fresh_kv, (0, 2, 1, 3))
    prev = jnp.transpose(prev_kv, (1, 0, 2))
    powers = jnp.transpose(exps, (1, 0, 2))
    q_parts = 3
    vmem = pl.BlockSpec(memory_space=pltpu.VMEM)
    anywhere = pl.BlockSpec(memory_space=pl.ANY)
    dma = pltpu.SemaphoreType.DMA
    return pl.pallas_call(
        functools.partial(kernel, rows, cols),
        out_shape=jax.ShapeDtypeStruct((STEPS, tok, half), BF16),
        in_specs=[anywhere, anywhere, vmem, vmem, vmem, anywhere],
        out_specs=vmem,
        scratch_shapes=[
            pltpu.VMEM((STEPS * tok, depth), BF16),
            pltpu.VMEM((q_parts, depth, width // q_parts), BF16),
            pltpu.VMEM((width, half), BF16),
            pltpu.VMEM((width, half), BF16),
            pltpu.VMEM((STEPS, tok, width), BF16),
            pltpu.VMEM((groups, STEPS, tok, width), BF16),
            pltpu.VMEM((2 * STEPS, QUAD + 1, tok, width), BF16),
            pltpu.VMEM((groups, heads, tok, QUAD * tok), BF16),
            pltpu.VMEM((tok, width), F32),
            pltpu.VMEM((tok, HD), F32),
            pltpu.VMEM((STEPS, groups, tok, width), BF16),
            pltpu.VMEM((STEPS, groups, tok, HD), F32),
            pltpu.VMEM((STEPS, groups, tok, width), BF16),
            pltpu.VMEM((STEPS, groups, tok, HD), F32),
            pltpu.VMEM((STEPS, tok, width), BF16),
            pltpu.VMEM((STEPS, tok, width), BF16),
            dma((2 + q_parts,)),
            dma((2 * STEPS, QUAD)),
            dma((2 * STEPS, QUAD)),
            dma,
            dma,
            dma((STEPS,)),
            dma((STEPS,)),
            dma((groups,)),
            dma((groups,)),
            dma((STEPS, groups)),
            dma((STEPS, groups)),
            dma((STEPS, groups)),
            dma((STEPS, groups)),
        ],
        compiler_params=pltpu.CompilerParams(
            collective_id=0, has_side_effects=True, vmem_limit_bytes=60 * 2**20
        ),
    )(hidden.reshape(STEPS * tok, depth), w_q, fresh, prev, powers, w_out)


def solution(mesh):
    rows, cols = grid_of(mesh.shape["patch"])
    return jax.shard_map(
        functools.partial(on_device, rows, cols),
        mesh=mesh,
        in_specs=(
            P(None, ("group", "patch"), None),
            P(None, "tensor"),
            P(None, ("group", "patch"), None, "tensor"),
            P(("group", "patch"), None, "tensor"),
            P(("group", "patch"), None, "tensor"),
            P("tensor", None),
        ),
        out_specs=P(None, ("group", "patch"), "tensor"),
        check_vma=False,
    )
```

```python
import functools

import jax
import jax.numpy as jnp
from jax import lax
from jax.experimental import pallas as pl
from jax.experimental.pallas import tpu as pltpu
from jax.sharding import PartitionSpec as P

HD = 128
STEPS = 2
CLIP = 1.0
MESH = pl.DeviceIdType.MESH
F32 = jnp.float32
BF16 = jnp.bfloat16
QUAD = 4
BY_ROW = ()


def grid_of(count):
    columns = 1
    while columns * columns * 4 <= count and count % (columns * 2) == 0:
        columns *= 2
    return count // columns, columns


def kernel(
    rows, cols,
    hidden, w_q, fresh, prev, exps, w_out,
    out,
    hid, wq, wo_own, wo_far, query, query_in, table, probs, own_sum, own_stat,
    part_out, stat_out, part_in, stat_in, att, att_far,
    local_sem, send_sem, recv_sem, core_send, core_recv, att_send, att_recv,
    query_send, query_recv, part_send, part_recv, stat_send, stat_recv,
):
    tok, width = prev.shape[0], prev.shape[2]
    heads = width // HD
    keys = QUAD * tok
    half = w_out.shape[1] // 2
    me = lax.axis_index("patch")
    core = lax.axis_index("tensor")
    row, col = me // cols, me % cols
    q_parts = wq.shape[0]
    groups = rows * cols // QUAD
    peers = range(1, groups)
    group = (row // 2) * (cols // 2) + col // 2
    row_peer = (row + 1 - 2 * (row % 2)) * cols + col
    col_peer = row * cols + col + 1 - 2 * (col % 2)

    def peer(j):
        to = lax.rem(group + j + groups, groups)
        return (2 * (to // (cols // 2)) + row % 2) * cols + 2 * (to % (cols // 2)) + col % 2

    barrier = pltpu.get_barrier_semaphore()
    for index in [row_peer, col_peer] + [peer(j) for j in peers]:
        pl.semaphore_signal(barrier, inc=1, device_id={"patch": index}, device_id_type=MESH)
    pl.semaphore_signal(barrier, inc=1, device_id={"tensor": 1 - core}, device_id_type=MESH)

    local = [pltpu.make_async_copy(hidden, hid, local_sem.at[0])]
    part = width // q_parts
    for j in range(q_parts):
        local.append(
            pltpu.make_async_copy(w_q.at[:, pl.ds(j * part, part)], wq.at[j], local_sem.at[1 + j])
        )
    mine = pl.ds(pl.multiple_of(core * half, half), half)
    theirs = pl.ds(pl.multiple_of((1 - core) * half, half), half)
    for copy in local:
        copy.start()
    wo_copy = pltpu.make_async_copy(w_out.at[:, mine], wo_own, local_sem.at[1 + q_parts])
    wo_copy.start()
    pl.semaphore_wait(barrier, groups + 2)

    def remote(src, chunk, slot, index):
        return pltpu.make_async_remote_copy(
            src_ref=src, dst_ref=table.at[chunk, slot],
            send_sem=send_sem.at[chunk, slot], recv_sem=recv_sem.at[chunk, slot],
            device_id={"patch": index}, device_id_type=MESH,
        )

    def own_copies(chunk):
        src = table.at[chunk, QUAD]
        return [remote(src, chunk, 2, col_peer), remote(src, chunk, 1, row_peer)]

    def onward(chunk):
        first, index = (2, row_peer) if chunk in BY_ROW else (1, col_peer)
        return first, remote(table.at[chunk, first], chunk, 3, index)

    def send_own(chunk):
        for copy in own_copies(chunk):
            copy.start()

    def forward(chunk):
        first, copy = onward(chunk)
        own_copies(chunk)[2 - first].wait_recv()
        copy.start()

    def complete(chunk):
        first, copy = onward(chunk)
        own_copies(chunk)[first - 1].wait_recv()
        copy.wait_recv()

    def drain():
        for chunk in range(2 * STEPS):
            for copy in own_copies(chunk) + [onward(chunk)[1]]:
                copy.wait_send()

    for kv in range(2):
        table[kv, QUAD] = prev[:, kv, :]
        send_own(kv)
    far_copy = pltpu.make_async_remote_copy(
        src_ref=w_out.at[:, theirs], dst_ref=wo_far,
        send_sem=core_send, recv_sem=core_recv,
        device_id={"tensor": 1 - core}, device_id_type=MESH,
    )
    far_copy.start()

    def query_copy(j):
        return pltpu.make_async_remote_copy(
            src_ref=query, dst_ref=query_in.at[j], send_sem=query_send.at[j], recv_sem=query_recv.at[j],
            device_id={"patch": peer(j)}, device_id_type=MESH,
        )

    def part_copies(step, j):
        return [
            pltpu.make_async_remote_copy(
                src_ref=src.at[step, j], dst_ref=dst.at[step, j],
                send_sem=send.at[step, j], recv_sem=recv.at[step, j],
                device_id={"patch": peer(-j)}, device_id_type=MESH,
            )
            for src, dst, send, recv in (
                (part_out, part_in, part_send, part_recv), (stat_out, stat_in, stat_send, stat_recv),
            )
        ]

    local[0].wait()
    for j in range(q_parts):
        local[1 + j].wait()
        result = jnp.dot(hid[...], wq[j], preferred_element_type=F32).astype(BF16)
        query[0, :, j * part:(j + 1) * part] = result[:tok]
        query[1, :, j * part:(j + 1) * part] = result[tok:]

    for j in peers:
        query_copy(j).start()

    for chunk in range(2 * STEPS):
        table[chunk, 0] = fresh[chunk // 2, :, chunk % 2, :]
    for kv in range(2):
        factors = jnp.exp2(-exps[:, kv, :].astype(F32)).T
        for h in range(heads):
            at = slice(h * HD, (h + 1) * HD)
            factor = factors[:, h:h + 1]
            old = table[kv, QUAD, :, at].astype(F32)
            scaled = jnp.clip((table[kv, 0, :, at].astype(F32) - old) * factor, -CLIP, CLIP).astype(BF16)
            update = (scaled.astype(F32) / factor).astype(BF16)
            table[2 + kv, QUAD, :, at] = (old + update.astype(F32)).astype(BF16)

    def at_head(h):
        return slice(h * HD, (h + 1) * HD)

    def weigh(step, h, j):
        other = not isinstance(j, int) or j > 0
        first = 1 if other else 0
        queries = query_in[j, step, :, at_head(h)] if other else query[step, :, at_head(h)]
        k_rows = table[2 * step, first:first + QUAD, :, at_head(h)].reshape(keys, HD)
        scores = lax.dot_general(
            queries, k_rows, (((1,), (1,)), ((), ())), preferred_element_type=F32
        ) * HD ** -0.5
        top = jnp.max(scores, axis=1, keepdims=True)
        e = jnp.exp(scores - top)
        probs[j, h] = e.astype(BF16)
        total = jnp.sum(e, axis=1, keepdims=True)
        if other:
            stat_out[step, j, :, h:h + 1] = top
            stat_out[step, j, :, heads + h:heads + h + 1] = total
        else:
            own_stat[:, h:h + 1] = top
            own_stat[:, heads + h:heads + h + 1] = total

    def mix_values(step, h, j):
        other = not isinstance(j, int) or j > 0
        first = 1 if other else 0
        v_rows = table[2 * step + 1, first:first + QUAD, :, at_head(h)].reshape(keys, HD)
        mixed = jnp.dot(probs[j, h], v_rows, preferred_element_type=F32)
        if other:
            total = stat_out[step, j, :, heads + h:heads + h + 1]
            part_out[step, j, :, at_head(h)] = (mixed / total).astype(BF16)
        else:
            own_sum[:, at_head(h)] = mixed

    def each_head(run, step, who):
        for j in who:
            for h in range(heads):
                run(step, h, j)

    def each_peer(runs, step):
        def body(j, carry):
            for run in runs:
                for h in range(heads):
                    run(step, h, j)
            return carry
        if groups == 2:
            body(1, 0)
        else:
            lax.fori_loop(1, groups, body, 0)

    def give_back(step):
        for j in peers:
            for copy in part_copies(step, j):
                copy.start()

    def merge(step):
        for j in peers:
            for copy in part_copies(step, j):
                copy.wait_recv()
        for h in range(heads):
            one, two = slice(h, h + 1), slice(heads + h, heads + h + 1)
            top = own_stat[:, one]
            for j in peers:
                top = jnp.maximum(top, stat_in[step, j, :, one])
            share = jnp.exp(own_stat[:, one] - top)
            below = own_stat[:, two] * share
            above = own_sum[:, at_head(h)] * share
            for j in peers:
                share = stat_in[step, j, :, two] * jnp.exp(stat_in[step, j, :, one] - top)
                below = below + share
                above = above + part_in[step, j, :, at_head(h)].astype(F32) * share
            att[step, :, at_head(h)] = (above / below).astype(BF16)

    def swap(step):
        return pltpu.make_async_remote_copy(
            src_ref=att.at[step], dst_ref=att_far.at[step],
            send_sem=att_send.at[step], recv_sem=att_recv.at[step],
            device_id={"tensor": 1 - core}, device_id_type=MESH,
        )

    tile = 512

    def project(step):
        swap(step).wait_recv()
        for j in range(half // tile):
            at = slice(j * tile, (j + 1) * tile)
            total = jnp.dot(att[step], wo_own[:, at], preferred_element_type=F32)
            total = total + jnp.dot(att_far[step], wo_far[:, at], preferred_element_type=F32)
            out[step, :, at] = total.astype(BF16)

    forward(0)
    send_own(2)
    forward(1)
    send_own(3)
    forward(2)
    complete(0)
    complete(1)
    for j in peers:
        query_copy(j).wait_recv()
    each_peer((weigh, mix_values), 0)
    give_back(0)
    forward(3)
    complete(2)
    each_peer((weigh,), 1)
    complete(3)
    each_peer((mix_values,), 1)
    give_back(1)
    each_head(weigh, 0, (0,))
    each_head(mix_values, 0, (0,))
    wo_copy.wait()
    far_copy.wait()
    merge(0)
    swap(0).start()
    each_head(weigh, 1, (0,))
    each_head(mix_values, 1, (0,))
    project(0)
    merge(1)
    swap(1).start()
    project(1)
    for step in range(STEPS):
        swap(step).wait_send()
        for j in peers:
            for copy in part_copies(step, j):
                copy.wait_send()
    for j in peers:
        query_copy(j).wait_send()
    drain()


def on_device(rows, cols, hidden, w_q, fresh_kv, prev_kv, exps, w_out):
    tok, width = hidden.shape[1], w_q.shape[1]
    depth, half = w_q.shape[0], w_out.shape[1] // 2
    heads = width // HD
    groups = rows * cols // QUAD
    powers = jnp.transpose(exps, (2, 1, 0))
    q_parts = 3
    vmem = pl.BlockSpec(memory_space=pltpu.VMEM)
    anywhere = pl.BlockSpec(memory_space=pl.ANY)
    dma = pltpu.SemaphoreType.DMA
    return pl.pallas_call(
        functools.partial(kernel, rows, cols),
        out_shape=jax.ShapeDtypeStruct((STEPS, tok, half), BF16),
        in_specs=[anywhere, anywhere, vmem, vmem, vmem, anywhere],
        out_specs=vmem,
        scratch_shapes=[
            pltpu.VMEM((STEPS * tok, depth), BF16),
            pltpu.VMEM((q_parts, depth, width // q_parts), BF16),
            pltpu.VMEM((width, half), BF16),
            pltpu.VMEM((width, half), BF16),
            pltpu.VMEM((STEPS, tok, width), BF16),
            pltpu.VMEM((groups, STEPS, tok, width), BF16),
            pltpu.VMEM((2 * STEPS, QUAD + 1, tok, width), BF16),
            pltpu.VMEM((groups, heads, tok, QUAD * tok), BF16),
            pltpu.VMEM((tok, width), F32),
            pltpu.VMEM((tok, HD), F32),
            pltpu.VMEM((STEPS, groups, tok, width), BF16),
            pltpu.VMEM((STEPS, groups, tok, HD), F32),
            pltpu.VMEM((STEPS, groups, tok, width), BF16),
            pltpu.VMEM((STEPS, groups, tok, HD), F32),
            pltpu.VMEM((STEPS, tok, width), BF16),
            pltpu.VMEM((STEPS, tok, width), BF16),
            dma((2 + q_parts,)),
            dma((2 * STEPS, QUAD)),
            dma((2 * STEPS, QUAD)),
            dma,
            dma,
            dma((STEPS,)),
            dma((STEPS,)),
            dma((groups,)),
            dma((groups,)),
            dma((STEPS, groups)),
            dma((STEPS, groups)),
            dma((STEPS, groups)),
            dma((STEPS, groups)),
        ],
        compiler_params=pltpu.CompilerParams(
            collective_id=0, has_side_effects=True, vmem_limit_bytes=60 * 2**20
        ),
    )(hidden.reshape(STEPS * tok, depth), w_q, fresh_kv, prev_kv, powers, w_out)


def solution(mesh):
    rows, cols = grid_of(mesh.shape["patch"])
    return jax.shard_map(
        functools.partial(on_device, rows, cols),
        mesh=mesh,
        in_specs=(
            P(None, ("group", "patch"), None),
            P(None, "tensor"),
            P(None, ("group", "patch"), None, "tensor"),
            P(("group", "patch"), None, "tensor"),
            P(("group", "patch"), None, "tensor"),
            P("tensor", None),
        ),
        out_specs=P(None, ("group", "patch"), "tensor"),
        check_vma=False,
    )
```
